256 devices in a mesh: role: 2 (over x_lo), fsdp: 16 (over z, core), dp: 8 (over y, x_hi).
Axes of the slice: x: 4 (x_hi: 2, x_lo: 2; x = x_hi * 2 + x_lo), y: 4, z: 8, core: 2. Of those that a mesh axis runs over, the one named last changes fastest.
Arguments:
- acts: bfloat16 [4096, 4096], P(('role', 'fsdp'), 'dp'), may hold values from -6 to 6
- cotangent: bfloat16 [4096, 16384], P('dp', ('role', 'fsdp')), may hold values from -6 to 6
- example_of: int32 [4096, 1], P('dp'), may hold values from 0 to 127
- stats_old: float32 [8, 32, 2, 512, 512], P('dp', ('role', 'fsdp')), may hold values from -2 to 4096, as said below
- stale_roots: float32 [8, 16, 2, 512, 512], P('dp', 'fsdp'), may hold values from -1 to 1, as said below
Outputs:
- update: float32 [4096, 16384], P('dp', ('role', 'fsdp'))
- new_stats: float32 [8, 32, 2, 512, 512], P('dp', ('role', 'fsdp'))
The draws below stay inside these ranges and needn't reach their ends.
Inputs may be any that keep to these rules, and one draw needn't show every extreme that they name: `example_of`: every example 0 .. 127 is named by at least one token. Each 512 x 512 matrix stats_old[i, j, k] is symmetric and positive definite. Each 512 x 512 matrix stale_roots[i, j, k] is symmetric and positive definite.
All inputs are finite; a program needn't handle non-finite values.
Results may differ from the reference program's by a relative error of at most 0.0028.
Values may be sent and summed in bfloat16 or wider, within the bound.
A program may use at most 128 MiB of HBM per device.

```python
import jax
import jax.numpy as jnp
from jax import lax

D = 4096
FF = 16384
B = 512
NEWTON = 3
TOKENS = 4096
EXAMPLES = 128
NRB = 8
NCB = 32


def dominant(key, lead, scale):
    first, second = jax.random.split(key)
    offdiag = jax.random.uniform(first, lead + (B, B), jnp.float32, -1.0, 1.0)
    lift = jax.random.uniform(second, lead + (B,), jnp.float32, 1.0, 2.0)
    symmetric = 0.5 * (offdiag + jnp.swapaxes(offdiag, -1, -2))
    identity = jnp.eye(B, dtype=jnp.float32)
    return scale * (symmetric * (1.0 - identity) + identity * (B * lift)[..., None])


def draw_stats_old(key, part):
    return dominant(jax.random.fold_in(key, 11), (NRB, NCB, 2), 2.0)


def draw_stale_roots(key, part):
    return dominant(jax.random.fold_in(key, 23), (NRB, NCB // 2, 2), 0.25 / B)


def block_levels(stream_key, dims, shards, smallest, high):
    def one(axis_at, blocks):
        heights = jax.random.uniform(jax.random.fold_in(jax.random.fold_in(stream_key, 6), axis_at), (blocks,), jnp.float32, smallest / len(shards), high / len(shards))
        return jnp.repeat(jnp.exp(heights), dims[axis_at] // blocks).reshape((-1,) + (1,) * (len(dims) - axis_at - 1))

    loudness = one(*shards[0])
    for cut in shards[1:]:
        loudness = loudness * one(*cut)
    return loudness


def different_ones(rng, rows, count, top, lift):
    sequence = jax.random.permutation(jax.random.fold_in(rng, 1), count)
    boost = sequence
    for power in range(3):
        boost = boost * boost // count
    boost = boost * lift // count
    tickets = jax.random.randint(jax.random.fold_in(rng, 2), (rows, count), 0, 4096) + boost
    fixed_rows = jax.random.permutation(jax.random.fold_in(rng, 3), rows)[jnp.arange(count) % rows]
    tickets = jnp.where(jnp.arange(rows)[:, None] == fixed_rows[None, :], 1 << 14, tickets)
    merit = tickets * count + jnp.arange(count)
    return lax.top_k(merit.astype(jnp.int32), top)[1].astype(jnp.int32)


def scatter_about(key, extent, scale, bound, shards=(), kind=jnp.bfloat16):
    values = scale * jax.random.normal(key, extent, jnp.float32)
    if shards:
        values = values * block_levels(key, extent, shards, -0.22, 0.18)
    return jnp.clip(values, -bound, bound).astype(kind)


def setup_inputs(seed: int = 0) -> dict:
    arg_keys = jax.random.split(jax.random.key(seed), 6)
    acts = scatter_about(arg_keys[0], (TOKENS, D), 1.0, 6.0, ((0, 32), (1, 8)))
    cotangent = scatter_about(arg_keys[1], (TOKENS, FF), 1.0, 6.0, ((0, 8), (1, 32)))
    example_of = different_ones(arg_keys[2], TOKENS, EXAMPLES, 1, 64)
    stats_old = draw_stats_old(jax.random.fold_in(arg_keys[5], 71), 0)
    stale_roots = draw_stale_roots(jax.random.fold_in(arg_keys[5], 71), 0)
    return {"acts": acts, "cotangent": cotangent, "example_of": example_of, "stats_old": stats_old, "stale_roots": stale_roots}


decay = 0.9
highest = lax.Precision.HIGHEST

def inverse_root(matrix):
    identity = jnp.eye(matrix.shape[-1], dtype=jnp.float32)
    scale = jnp.sqrt(jnp.sum(matrix * matrix))
    current = matrix / scale
    root = identity * scale ** (-0.25)
    for iteration in range(NEWTON):
        factor = (5.0 * identity - current) * 0.25
        root = jnp.dot(root, factor, precision=highest, preferred_element_type=jnp.float32)
        if iteration + 1 < NEWTON:
            square = jnp.dot(factor, factor, precision=highest, preferred_element_type=jnp.float32)
            fourth = jnp.dot(square, square, precision=highest, preferred_element_type=jnp.float32)
            current = jnp.dot(fourth, current, precision=highest, preferred_element_type=jnp.float32)
    return root

def reference(acts, cotangent, example_of, stats_old, stale_roots):
    labels = jnp.arange(EXAMPLES, dtype=jnp.int32)
    onehot = (example_of[:, 0][:, None] == labels[None, :]).astype(jnp.float32)
    counts = lax.optimization_barrier(jnp.sum(onehot, axis=0))
    weight = lax.optimization_barrier(jnp.sum(onehot * (1.0 / counts)[None, :], axis=1))
    scaled = (cotangent.astype(jnp.float32) * weight[:, None]).astype(jnp.bfloat16)
    grad = lax.dot_general(acts, scaled, (((0,), (0,)), ((), ())), preferred_element_type=jnp.float32)
    blocks = grad.reshape(NRB, B, NCB, B).transpose(0, 2, 1, 3)
    left = decay * stats_old[:, :, 0] + (1.0 - decay) * jnp.einsum('ijab,ijcb->ijac', blocks, blocks, precision=highest)
    right = decay * stats_old[:, :, 1] + (1.0 - decay) * jnp.einsum('ijba,ijbc->ijac', blocks, blocks, precision=highest)
    new_stats = jnp.stack([left, right], axis=2)
    half = NCB // 2
    fresh_left = lax.map(inverse_root, left[:, half:].reshape(-1, B, B)).reshape(NRB, half, B, B)
    fresh_right = lax.map(inverse_root, right[:, half:].reshape(-1, B, B)).reshape(NRB, half, B, B)
    root_left = jnp.concatenate([stale_roots[:, :, 0], fresh_left], axis=1)
    root_right = jnp.concatenate([stale_roots[:, :, 1], fresh_right], axis=1)
    inner = jnp.einsum('ijab,ijbc->ijac', root_left, blocks, precision=highest)
    product = jnp.einsum('ijab,ijbc->ijac', inner, root_right, precision=highest)
    grad_size = jnp.sqrt(lax.optimization_barrier(jnp.mean(blocks * blocks, axis=(2, 3))))
    prod_size = jnp.sqrt(lax.optimization_barrier(jnp.mean(product * product, axis=(2, 3))) + 1e-06)
    update_blocks = product * (grad_size / prod_size)[:, :, None, None]
    update = update_blocks.transpose(0, 2, 1, 3).reshape(D, FF)
    return (update, new_stats)
```

```python
import functools

import jax
import jax.numpy as jnp
from jax import lax
from jax.experimental import pallas as pl
from jax.experimental.pallas import tpu as pltpu
from jax.sharding import PartitionSpec as P

MESH = pl.DeviceIdType.MESH
F32 = jnp.float32
BF16 = jnp.bfloat16
B = 512
Q = 128
EXAMPLES = 128
MIB = 1 << 20


def contract(left, right, left_dim, right_dim):
    return lax.dot_general(
        left, right, (((left_dim,), (right_dim,)), ((), ())), preferred_element_type=F32
    )


class Names:
    def __init__(self):
        self.table = {}

    def __call__(self, *key):
        return self.table.setdefault(key, len(self.table))


COPIES = 96


def gather_kernel(
    acts_ref, cot_ref, ids_ref, grad_ref, acts_all, cot_all, ids_all, weights, local_sem, send_sem, recv_sem
):
    role = lax.axis_index("role")
    fsdp = lax.axis_index("fsdp")
    dp = lax.axis_index("dp")
    z, core = fsdp // 2, fsdp % 2
    y, half = dp // 2, dp % 2
    number = Names()

    def device(role=role, z=z, core=core, y=y, half=half):
        return (role, z * 2 + core, y * 2 + half)

    across = device(half=1 - half)
    y_up, y_down = device(y=(y + 1) % 4), device(y=(y + 3) % 4)
    z_up, z_down = device(z=(z + 1) % 8), device(z=(z + 7) % 8)
    partner = device(role=1 - role)
    sibling = device(core=1 - core)
    row_peers = [(role, fsdp, (dp + step) % 8) for step in range(1, 8)]

    def acts_block(block_role, block_z, block_core):
        index = block_role * 16 + block_z * 2 + block_core
        return acts_all.at[index // 4, pl.ds(pl.multiple_of((index % 4) * Q, Q), Q)]

    def cot_part(block_y, block_half, quarter):
        return cot_all.at[block_y * 2 + block_half, pl.ds(quarter * Q, Q)]

    sent = []

    def send(ref, key, target):
        index = number(*key)
        copy = pltpu.make_async_remote_copy(
            src_ref=ref,
            dst_ref=ref,
            send_sem=send_sem.at[index],
            recv_sem=recv_sem.at[index],
            device_id=target,
            device_id_type=MESH,
        )
        copy.start()
        sent.append(copy)

    def arrived(ref, key):
        index = number(*key)
        pltpu.make_async_remote_copy(
            src_ref=ref,
            dst_ref=ref,
            send_sem=send_sem.at[index],
            recv_sem=recv_sem.at[index],
            device_id=sibling,
            device_id_type=MESH,
        ).wait_recv()

    own_acts = acts_block(role, z, core)
    own_cot = cot_all.at[dp]
    local = [
        pltpu.make_async_copy(ids_ref, ids_all.at[dp], local_sem.at[0]),
        pltpu.make_async_copy(acts_ref, own_acts, local_sem.at[1]),
        pltpu.make_async_copy(cot_ref, own_cot, local_sem.at[2]),
    ]
    for copy in local:
        copy.start()

    barrier = pltpu.get_barrier_semaphore()
    others = [y_up, y_down, across] + [
        device(y=(y + 1) % 4, half=1 - half),
        device(y=(y + 3) % 4, half=1 - half),
        device(y=(y + 2) % 4),
        device(y=(y + 2) % 4, half=1 - half),
    ]
    everyone = others + [z_up, z_down, partner, sibling]
    for target in everyone:
        pl.semaphore_signal(barrier, inc=1, device_id=target, device_id_type=MESH)
    for copy in local:
        copy.wait()
    pl.semaphore_wait(barrier, len(everyone))

    for step, target in enumerate(row_peers, 1):
        send(ids_all.at[dp], ("ids", step), target)
    send(own_acts, ("partner",), partner)
    send(own_acts, ("up", 0, 1), z_up)
    send(own_acts, ("down", 0, 1), z_down)

    def own(quarter, direction):
        send(cot_part(y, half, quarter), ("y", direction, 0, quarter), y_up if direction else y_down)

    own(0, 1)
    own(3, 0)
    for quarter in (0, 3):
        send(cot_part(y, half, quarter), ("x", 0, quarter), across)
    own(1, 1)
    own(2, 0)
    for quarter in (1, 2):
        send(cot_part(y, half, quarter), ("x", 0, quarter), across)
    own(2, 1)
    own(1, 0)
    send(own_acts, ("sibling", 0, 0), sibling)

    for step in range(1, 8):
        arrived(ids_all.at[(dp + 8 - step) % 8], ("ids", step))

    def onehot(block):
        labels = lax.broadcasted_iota(jnp.int32, (EXAMPLES, B), 0)
        return jnp.where(ids_all[block] == labels, 1.0, 0.0)

    seen = onehot(0)
    for block in range(1, 8):
        seen += onehot(block)
    inverse = jnp.broadcast_to(1.0 / jnp.sum(seen, axis=1, keepdims=True), (EXAMPLES, Q))
    high = inverse.astype(BF16)
    rest = inverse - high.astype(F32)
    middle = rest.astype(BF16)
    low = (rest - middle.astype(F32)).astype(BF16)
    split = jnp.concatenate([high, middle, low], axis=1)

    def weigh(block):
        spread = contract(onehot(block).astype(BF16), split, 0, 0)
        weights[block] = (spread[:, :Q] + spread[:, Q : 2 * Q]) + spread[:, 2 * Q :]

    def step_acts(stream, hop, last=False):
        stream_role = role if stream == 0 else 1 - role
        for key, sign, target in (("up", -1, z_up), ("down", 1, z_down)):
            if hop == 4 and stream != (0 if key == "up" else 1):
                continue
            block = acts_block(stream_role, (z + 8 + sign * hop) % 8, core)
            arrived(block, (key, stream, hop))
            if hop < 3 or (hop == 3 and stream == (0 if key == "up" else 1)):
                send(block, (key, stream, hop + 1), target)
            send(block, ("sibling", stream, (8 + sign * hop) % 8), sibling)

    block = acts_block(1 - role, z, core)
    arrived(block, ("partner",))
    send(block, ("up", 1, 1), z_up)
    send(block, ("down", 1, 1), z_down)
    send(block, ("sibling", 1, 0), sibling)
    step_acts(0, 1)

    up_y, down_y, far_y = (y + 1) % 4, (y + 3) % 4, (y + 2) % 4
    for first, second in ((0, 3), (1, 2)):
        part = cot_part(down_y, half, first)
        arrived(part, ("y", 1, 0, first))
        send(part, ("y", 1, 1, first), y_up)
        part = cot_part(up_y, half, second)
        arrived(part, ("y", 0, 0, second))
        send(part, ("y", 0, 1, second), y_down)
    own(3, 1)
    own(0, 0)

    step_acts(1, 1)
    step_acts(0, 2)
    for quarter in (0, 3, 1, 2):
        part = cot_part(y, 1 - half, quarter)
        arrived(part, ("x", 0, quarter))
        send(part, ("y", 1, 2, quarter), y_up)
        send(part, ("y", 0, 2, quarter), y_down)
    step_acts(1, 2)
    for quarters in ((0, 3), (1, 2)):
        for quarter in quarters:
            part = cot_part(far_y, half, quarter)
            arrived(part, ("y", 1 if quarter < 2 else 0, 1, quarter))
            send(part, ("x", 1, quarter), across)
    step_acts(0, 3)
    step_acts(1, 3)

    for block in range(8):
        weigh(block)

    for quarter in (2, 3):
        arrived(cot_part(down_y, half, quarter), ("y", 1, 0, quarter))
    for quarter in (0, 1):
        arrived(cot_part(up_y, half, quarter), ("y", 0, 0, quarter))
    step_acts(0, 4)
    step_acts(1, 4)
    for stream in range(2):
        stream_role = role if stream == 0 else 1 - role
        for offset in range(8):
            arrived(acts_block(stream_role, (z + offset) % 8, 1 - core), ("sibling", stream, offset))

    def product(block, start, size):
        rows = pl.ds(start, size)
        weight = weights[block, rows]
        scaled = jnp.concatenate(
            [
                (cot_all[block, rows, pl.ds(lane, Q)].astype(F32) * weight).astype(BF16)
                for lane in range(0, B, Q)
            ],
            axis=1,
        )
        return contract(acts_all[block, rows], scaled, 0, 0)

    grad_ref[...] = product(dp, 0, B)
    for block in (down_y * 2 + half, up_y * 2 + half, y * 2 + 1 - half, far_y * 2 + half):
        grad_ref[...] += product(block, 0, B)
    for quarters, start in (((0, 3), None), ((1, 2), None)):
        for quarter in quarters:
            arrived(cot_part(down_y, 1 - half, quarter), ("y", 1, 2, quarter))
            grad_ref[...] += product(down_y * 2 + 1 - half, quarter * Q, Q)
            arrived(cot_part(up_y, 1 - half, quarter), ("y", 0, 2, quarter))
            grad_ref[...] += product(up_y * 2 + 1 - half, quarter * Q, Q)
            arrived(cot_part(far_y, 1 - half, quarter), ("x", 1, quarter))
            grad_ref[...] += product(far_y * 2 + 1 - half, quarter * Q, Q)

    for copy in sent:
        copy.wait_send()
    assert len(number.table) <= COPIES


def gather(acts, cotangent, ids):
    return pl.pallas_call(
        gather_kernel,
        out_shape=jax.ShapeDtypeStruct((B, B), F32),
        in_specs=[pl.BlockSpec(memory_space=pl.ANY)] * 3,
        out_specs=pl.BlockSpec(memory_space=pltpu.VMEM),
        scratch_shapes=[
            pltpu.VMEM((8, B, B), BF16),
            pltpu.VMEM((8, B, B), BF16),
            pltpu.VMEM((8, 1, B), jnp.int32),
            pltpu.VMEM((8, B, Q), F32),
            pltpu.SemaphoreType.DMA((3,)),
            pltpu.SemaphoreType.DMA((COPIES,)),
            pltpu.SemaphoreType.DMA((COPIES,)),
        ],
        compiler_params=pltpu.CompilerParams(
            collective_id=0, has_side_effects=True, vmem_limit_bytes=24 * MIB
        ),
    )(acts, cotangent, ids)


def parts_of(matrix):
    high = matrix.astype(BF16)
    return high, (matrix - high.astype(F32)).astype(BF16)


def precise(left, right, left_dim, right_dim):
    (left_high, left_low), (right_high, right_low) = left, right
    return contract(
        jnp.concatenate([left_high, left_low, left_high], axis=left_dim),
        jnp.concatenate([right_high, right_high, right_low], axis=right_dim),
        left_dim,
        right_dim,
    )


def rough(left, right):
    return contract(left.astype(BF16), right.astype(BF16), 1, 0)


def total(matrix):
    return jnp.sum(jnp.sum(matrix, axis=0, keepdims=True), axis=1, keepdims=True)


def block_kernel(
    grad_ref, stats_ref, stale_ref, update_ref, new_ref, grad, stats, stale, fresh, update, apart, load_sem, store_sem
):
    role = lax.axis_index("role")
    loads = [
        pltpu.make_async_copy(grad_ref, grad, load_sem.at[0]),
        pltpu.make_async_copy(stats_ref.at[0, 0, 0], stats.at[0], load_sem.at[1]),
        pltpu.make_async_copy(stats_ref.at[0, 0, 1], stats.at[1], load_sem.at[2]),
    ]
    for copy in loads:
        copy.start()
    stale_load = pltpu.make_async_copy(stale_ref.at[0, 0], stale, load_sem.at[3])
    stale_load.start()
    stores = [
        pltpu.make_async_copy(fresh.at[0], new_ref.at[0, 0, 0], store_sem.at[0]),
        pltpu.make_async_copy(fresh.at[1], new_ref.at[0, 0, 1], store_sem.at[1]),
    ]
    loads[0].wait()
    halves = parts_of(grad[...])
    for side in range(2):
        gram = precise(halves, halves, 1 - side, 1 - side)
        loads[1 + side].wait()
        fresh[side] = 0.9 * stats[side] + (1.0 - 0.9) * gram
        stores[side].start()
    stale_load.wait()

    @pl.when(role == 0)
    def _():
        inner = precise(parts_of(stale[0]), halves, 1, 0)
        update[...] = precise(parts_of(inner), parts_of(stale[1]), 1, 0)

    @pl.when(role == 1)
    def _():
        square = [total(fresh[side] * fresh[side]) for side in range(2)]
        stats[0] = fresh[0] * lax.rsqrt(square[0])
        stats[1] = fresh[1] * lax.rsqrt(square[1])
        for side in range(2):
            m = stats[side]
            m2 = rough(m, m)
            m3 = rough(m, m2)
            n = (625.0 / 256) * m - (500.0 / 256) * m2 + (150.0 / 256) * m3
            n += rough(m3, (1.0 / 256) * m2 - (20.0 / 256) * m)
            n2 = rough(n, n)
            n3 = rough(n, n2)
            g = (-5.0 / 16 - 3125.0 / 4096) * n + (3125.0 / 4096) * n2 - (1250.0 / 4096) * n3
            g += rough(n3, (250.0 / 4096) * n - (25.0 / 4096) * n2 + (1.0 / 4096) * n3)
            apart[side] = 1.25 * g - (25.0 / 64) * m - 0.25 * rough(m, g)
        scale = [lax.rsqrt(jnp.sqrt(jnp.sqrt(value))) for value in square]
        whole = grad[...]
        inner = (125.0 / 64) * whole + rough(apart[0], whole)
        product = (125.0 / 64) * inner + rough(inner, apart[1])
        update[...] = product * (scale[0] * scale[1])

    whole = grad[...]
    grad_size = jnp.sqrt(total(whole * whole) * (1.0 / (B * B)))
    product = update[...]
    prod_size = jnp.sqrt(total(product * product) * (1.0 / (B * B)) + 1e-06)
    update[...] = product * (grad_size / prod_size)
    last = pltpu.make_async_copy(update, update_ref, store_sem.at[2])
    last.start()
    for copy in stores:
        copy.wait()
    last.wait()


def block_step(grad, stats_old, stale_roots):
    return pl.pallas_call(
        block_kernel,
        out_shape=(
            jax.ShapeDtypeStruct((B, B), F32),
            jax.ShapeDtypeStruct((1, 1, 2, B, B), F32),
        ),
        in_specs=[pl.BlockSpec(memory_space=pl.ANY)] * 3,
        out_specs=(pl.BlockSpec(memory_space=pl.ANY),) * 2,
        scratch_shapes=[
            pltpu.VMEM((B, B), F32),
            pltpu.VMEM((2, B, B), F32),
            pltpu.VMEM((2, B, B), F32),
            pltpu.VMEM((2, B, B), F32),
            pltpu.VMEM((B, B), F32),
            pltpu.VMEM((2, B, B), F32),
            pltpu.SemaphoreType.DMA((4,)),
            pltpu.SemaphoreType.DMA((3,)),
        ],
        compiler_params=pltpu.CompilerParams(vmem_limit_bytes=32 * MIB),
    )(grad, stats_old, stale_roots)


def shards(acts, cotangent, example_of, stats_old, stale_roots):
    grad = gather(acts, cotangent, example_of.reshape(1, B))
    return block_step(grad, stats_old, stale_roots)


def solution(mesh):
    return jax.shard_map(
        shards,
        mesh=mesh,
        in_specs=(
            P(("role", "fsdp"), "dp"),
            P("dp", ("role", "fsdp")),
            P("dp", None),
            P("dp", ("role", "fsdp"), None, None, None),
            P("dp", "fsdp", None, None, None),
        ),
        out_specs=(P("dp", ("role", "fsdp")), P("dp", ("role", "fsdp"), None, None, None)),
        check_vma=False,
    )
```

```python
import functools

import jax
import jax.numpy as jnp
from jax import lax
from jax.experimental import pallas as pl
from jax.experimental.pallas import tpu as pltpu
from jax.sharding import PartitionSpec as P

MESH = pl.DeviceIdType.MESH
F32 = jnp.float32
BF16 = jnp.bfloat16
B = 512
Q = 128
EXAMPLES = 128
MIB = 1 << 20


def contract(left, right, left_dim, right_dim):
    return lax.dot_general(
        left, right, (((left_dim,), (right_dim,)), ((), ())), preferred_element_type=F32
    )


class Names:
    def __init__(self):
        self.table = {}

    def __call__(self, *key):
        return self.table.setdefault(key, len(self.table))


COPIES = 96


def gather_kernel(
    acts_ref,
    cot_ref,
    ids_ref,
    stats_ref,
    stale_ref,
    grad_ref,
    stats_out,
    stale_out,
    acts_all,
    cot_all,
    ids_all,
    weights,
    local_sem,
    send_sem,
    recv_sem,
):
    role = lax.axis_index("role")
    fsdp = lax.axis_index("fsdp")
    dp = lax.axis_index("dp")
    z, core = fsdp // 2, fsdp % 2
    y, half = dp // 2, dp % 2
    number = Names()

    def device(role=role, z=z, core=core, y=y, half=half):
        return (role, z * 2 + core, y * 2 + half)

    across = device(half=1 - half)
    y_up, y_down = device(y=(y + 1) % 4), device(y=(y + 3) % 4)
    z_up, z_down = device(z=(z + 1) % 8), device(z=(z + 7) % 8)
    partner = device(role=1 - role)
    sibling = device(core=1 - core)
    row_peers = [(role, fsdp, (dp + step) % 8) for step in range(1, 8)]

    def acts_block(block_role, block_z, block_core):
        index = block_role * 16 + block_z * 2 + block_core
        return acts_all.at[index // 4, pl.ds(pl.multiple_of((index % 4) * Q, Q), Q)]

    def cot_part(block_y, block_half, quarter):
        return cot_all.at[block_y * 2 + block_half, pl.ds(quarter * Q, Q)]

    sent = []

    def copy_of(ref, key, target):
        index = number(*key)
        return pltpu.make_async_remote_copy(
            src_ref=ref,
            dst_ref=ref,
            send_sem=send_sem.at[index],
            recv_sem=recv_sem.at[index],
            device_id=target,
            device_id_type=MESH,
        )

    def send(ref, key, target):
        copy = copy_of(ref, key, target)
        copy.start()
        sent.append(copy)

    def arrived(ref, key):
        copy_of(ref, key, sibling).wait_recv()

    own_acts = acts_block(role, z, core)
    own_cot = cot_all.at[dp]
    local = [
        pltpu.make_async_copy(ids_ref, ids_all.at[dp], local_sem.at[0]),
        pltpu.make_async_copy(acts_ref, own_acts, local_sem.at[1]),
        pltpu.make_async_copy(cot_ref, own_cot, local_sem.at[2]),
    ]
    for copy in local:
        copy.start()

    barrier = pltpu.get_barrier_semaphore()
    others = [y_up, y_down, across] + [
        device(y=(y + 1) % 4, half=1 - half),
        device(y=(y + 3) % 4, half=1 - half),
        device(y=(y + 2) % 4),
        device(y=(y + 2) % 4, half=1 - half),
    ]
    everyone = others + [z_up, z_down, partner, sibling]
    for target in everyone:
        pl.semaphore_signal(barrier, inc=1, device_id=target, device_id_type=MESH)
    for copy in local:
        copy.wait()
    ahead = [
        pltpu.make_async_copy(stats_ref.at[0, 0], stats_out, local_sem.at[3]),
        pltpu.make_async_copy(stale_ref.at[0, 0], stale_out, local_sem.at[4]),
    ]
    for copy in ahead:
        copy.start()
    pl.semaphore_wait(barrier, len(everyone))

    for step, target in enumerate(row_peers, 1):
        send(ids_all.at[dp], ("ids", step), target)
    send(own_acts, ("partner",), partner)
    send(own_acts, ("up", 0, 1), z_up)
    send(own_acts, ("down", 0, 1), z_down)

    def own(quarter, direction):
        send(cot_part(y, half, quarter), ("y", direction, 0, quarter), y_up if direction else y_down)

    for pair in ((0, 3), (1, 2)):
        own(pair[0], 1)
        own(pair[1], 0)
        for quarter in pair:
            send(cot_part(y, half, quarter), ("x", 0, quarter), across)
    send(own_acts, ("sibling", 0, 0), sibling)

    for step in range(1, 8):
        arrived(ids_all.at[(dp + 8 - step) % 8], ("ids", step))

    def onehot(block):
        labels = lax.broadcasted_iota(jnp.int32, (EXAMPLES, B), 0)
        return jnp.where(ids_all[block] == labels, 1.0, 0.0)

    seen = lax.fori_loop(1, 8, lambda block, seen: seen + onehot(block), onehot(0))
    inverse = jnp.broadcast_to(1.0 / jnp.sum(seen, axis=1, keepdims=True), (EXAMPLES, Q))
    high = inverse.astype(BF16)
    rest = inverse - high.astype(F32)
    middle = rest.astype(BF16)
    low = (rest - middle.astype(F32)).astype(BF16)
    split = jnp.concatenate([high, middle, low], axis=1)

    def weigh(block, carry):
        spread = contract(onehot(block).astype(BF16), split, 0, 0)
        weights[block] = (spread[:, :Q] + spread[:, Q : 2 * Q]) + spread[:, 2 * Q :]
        return carry

    def step_acts(stream, hop):
        stream_role = role if stream == 0 else 1 - role
        for key, sign, target in (("up", -1, z_up), ("down", 1, z_down)):
            if hop == 4 and stream != (0 if key == "up" else 1):
                continue
            block = acts_block(stream_role, (z + 8 + sign * hop) % 8, core)
            arrived(block, (key, stream, hop))
            if hop < 3 or (hop == 3 and stream == (0 if key == "up" else 1)):
                send(block, (key, stream, hop + 1), target)
            send(block, ("sibling", stream, (8 + sign * hop) % 8), sibling)

    def from_sibling(offset):
        for stream in range(2):
            stream_role = role if stream == 0 else 1 - role
            arrived(acts_block(stream_role, (z + offset) % 8, 1 - core), ("sibling", stream, offset))

    up_y, down_y, far_y = (y + 1) % 4, (y + 3) % 4, (y + 2) % 4

    def pass_on(first, second):
        part = cot_part(down_y, half, first)
        arrived(part, ("y", 1, 0, first))
        send(part, ("y", 1, 1, first), y_up)
        part = cot_part(up_y, half, second)
        arrived(part, ("y", 0, 0, second))
        send(part, ("y", 0, 1, second), y_down)

    far = [copy_of(cot_part(far_y, half, quarter), ("x", 1, quarter), across) for quarter in (0, 3, 1, 2)]

    def send_far(*which):
        def start():
            for index in which:
                far[index].start()

        return start

    def far_arrived(*quarters):
        for quarter in quarters:
            arrived(cot_part(far_y, half, quarter), ("y", 1 if quarter < 2 else 0, 1, quarter))

    pass_on(0, 3)
    block = acts_block(1 - role, z, core)
    arrived(block, ("partner",))
    send(block, ("up", 1, 1), z_up)
    send(block, ("down", 1, 1), z_down)
    send(block, ("sibling", 1, 0), sibling)
    step_acts(0, 1)
    pass_on(1, 2)
    for quarter in (2, 3):
        own(quarter, 1)
        own(3 - quarter, 0)

    step_acts(1, 1)
    far_arrived(0, 3)
    send_far(0, 1)()
    far_arrived(1, 2)
    send_far(2, 3)()
    step_acts(0, 2)
    for quarter in (0, 3, 1):
        part = cot_part(y, 1 - half, quarter)
        arrived(part, ("x", 0, quarter))
        send(part, ("y", 1, 2, quarter), y_up)
        send(part, ("y", 0, 2, quarter), y_down)
    arrived(cot_part(y, 1 - half, 2), ("x", 0, 2))
    arrived(cot_part(down_y, half, 2), ("y", 1, 0, 2))
    send(
        cot_part(y, 1 - half, 2),
        ("y", 1, 2, 2),
        y_up,
    )
    send(
        cot_part(y, 1 - half, 2),
        ("y", 0, 2, 2),
        y_down,
    )
    step_acts(1, 2)
    lax.fori_loop(0, 8, weigh, 0)
    step_acts(0, 3)

    def wait_y(quarter):
        arrived(cot_part(down_y, 1 - half, quarter), ("y", 1, 2, quarter))
        arrived(cot_part(up_y, 1 - half, quarter), ("y", 0, 2, quarter))

    wait_y(0)
    step_acts(1, 3)

    arrived(cot_part(down_y, half, 3), ("y", 1, 0, 3))
    for quarter in (0, 1):
        arrived(cot_part(up_y, half, quarter), ("y", 0, 0, quarter))

    def scaled(block, rows):
        weight = weights[block, rows]
        return jnp.concatenate(
            [
                (cot_all[block, rows, pl.ds(lane, Q)].astype(F32) * weight).astype(BF16)
                for lane in range(0, B, Q)
            ],
            axis=1,
        )

    def early(index, carry):
        block_z = (z + index // 2 + 5) % 8
        block = index % 2 * 4 + block_z // 2
        rows = pl.ds(pl.multiple_of(block_z % 2 * (2 * Q), 2 * Q), 2 * Q)

        @pl.when(jnp.logical_or(block % 2 == half, block // 2 == y))
        def _():
            grad_ref[...] += contract(acts_all[block, rows], scaled(block, rows), 0, 0)

        return carry

    grad_ref[...] = jnp.zeros((B, B), F32)
    for offset in range(8):
        if offset != 4:
            from_sibling(offset)
    lax.fori_loop(0, 14, early, 0)
    step_acts(0, 4)
    step_acts(1, 4)
    from_sibling(4)
    lax.fori_loop(14, 16, early, 0)

    late = [block_y * 2 + 1 - half for block_y in (down_y, up_y, far_y)]
    for quarter in (0, 3, 1, 2):
        if quarter != 0:
            wait_y(quarter)
        arrived(cot_part(far_y, 1 - half, quarter), ("x", 1, quarter))
        rows = pl.ds(quarter * Q, Q)
        grad_ref[...] += contract(
            jnp.concatenate([acts_all[block, rows] for block in late], axis=0),
            jnp.concatenate([scaled(block, rows) for block in late], axis=0),
            0,
            0,
        )

    for copy in ahead:
        copy.wait()
    for copy in sent + far:
        copy.wait_send()
    assert len(number.table) <= COPIES


def gather(*operands):
    operands = [pltpu.with_memory_space_constraint(operand, pltpu.HBM) for operand in operands]
    return pl.pallas_call(
        gather_kernel,
        out_shape=(
            pltpu.VMEM((B, B), F32),
            pltpu.VMEM((2, B, B), F32),
            pltpu.VMEM((2, B, B), F32),
        ),
        in_specs=[pl.BlockSpec(memory_space=pltpu.HBM)] * 5,
        out_specs=(pl.BlockSpec(memory_space=pltpu.VMEM),) * 3,
        scratch_shapes=[
            pltpu.VMEM((8, B, B), BF16),
            pltpu.VMEM((8, B, B), BF16),
            pltpu.VMEM((8, 1, B), jnp.int32),
            pltpu.VMEM((8, B, Q), F32),
            pltpu.SemaphoreType.DMA((5,)),
            pltpu.SemaphoreType.DMA((COPIES,)),
            pltpu.SemaphoreType.DMA((COPIES,)),
        ],
        compiler_params=pltpu.CompilerParams(
            collective_id=0, has_side_effects=True, vmem_limit_bytes=24 * MIB
        ),
    )(*operands)


def parts_of(matrix):
    high = matrix.astype(BF16)
    return high, (matrix - high.astype(F32)).astype(BF16)


def precise(left, right, left_dim, right_dim):
    (left_high, left_low), (right_high, right_low) = left, right
    return contract(
        jnp.concatenate([left_high, left_low, left_high], axis=left_dim),
        jnp.concatenate([right_high, right_high, right_low], axis=right_dim),
        left_dim,
        right_dim,
    )


def rough(left, right):
    return contract(left.astype(BF16), right.astype(BF16), 1, 0)


def total(matrix):
    return jnp.sum(jnp.sum(matrix, axis=0, keepdims=True), axis=1, keepdims=True)


def block_kernel(
    grad, stats, stale, update_ref, new_ref, fresh, update, store_sem
):
    role = lax.axis_index("role")
    stores = [
        pltpu.make_async_copy(fresh.at[0], new_ref.at[0, 0, 0], store_sem.at[0]),
        pltpu.make_async_copy(fresh.at[1], new_ref.at[0, 0, 1], store_sem.at[1]),
    ]
    whole = grad[...]
    halves = parts_of(whole)
    for side in range(2):
        gram = contract(halves[0], halves[0], 1 - side, 1 - side)
        fresh[side] = 0.9 * stats[side] + (1.0 - 0.9) * gram
        stores[side].start()

    @pl.when(role == 0)
    def _():
        inner = precise(parts_of(stale[0]), halves, 1, 0)
        update[...] = precise(parts_of(inner), parts_of(stale[1]), 1, 0)

    @pl.when(role == 1)
    def _():
        sides = range(2)
        a = [fresh[side].astype(BF16) for side in sides]
        square = [total(fresh[side] * fresh[side]) for side in sides]
        r = [lax.rsqrt(square[side]) for side in sides]
        m2 = [(r[side] * r[side]) * rough(a[side], a[side]) for side in sides]
        m3 = [r[side] * rough(a[side], m2[side]) for side in sides]
        m4 = [(1.0 / 256) * m2[side] - (20.0 / 256) * r[side] * fresh[side] for side in sides]
        n = [
            (625.0 / 256) * r[side] * fresh[side]
            - (500.0 / 256) * m2[side]
            + (150.0 / 256) * m3[side]
            + rough(m3[side], m4[side])
            for side in sides
        ]
        n2 = [rough(n[side], n[side]) for side in sides]
        n3 = [rough(n[side], n2[side]) for side in sides]
        n4 = [
            (250.0 / 4096) * n[side] - (25.0 / 4096) * n2[side] + (1.0 / 4096) * n3[side] for side in sides
        ]
        g = [
            (-5.0 / 16 - 3125.0 / 4096) * n[side]
            + (3125.0 / 4096) * n2[side]
            - (1250.0 / 4096) * n3[side]
            + rough(n3[side], n4[side])
            for side in sides
        ]
        apart = [
            1.25 * g[side] - r[side] * ((25.0 / 64) * fresh[side] + 0.25 * rough(a[side], g[side]))
            for side in sides
        ]
        scale = [lax.rsqrt(jnp.sqrt(jnp.sqrt(value))) for value in square]
        inner = (125.0 / 64) * grad[...] + rough(apart[0], grad[...])
        product = (125.0 / 64) * inner + rough(inner, apart[1])
        update[...] = product * (scale[0] * scale[1])

    grad_size = jnp.sqrt(total(grad[...] * grad[...]) * (1.0 / (B * B)))
    prod_size = jnp.sqrt(total(update[...] * update[...]) * (1.0 / (B * B)) + 1e-06)
    ratio = grad_size / prod_size
    for part in range(4):
        rows = pl.ds(part * Q, Q)
        update[rows] = update[rows] * ratio
        copy = pltpu.make_async_copy(update.at[rows], update_ref.at[rows], store_sem.at[2 + part])
        copy.start()
        stores.append(copy)
    for copy in stores:
        copy.wait()


def block_step(grad, stats_old, stale_roots):
    return pl.pallas_call(
        block_kernel,
        out_shape=(
            jax.ShapeDtypeStruct((B, B), F32),
            jax.ShapeDtypeStruct((1, 1, 2, B, B), F32),
        ),
        in_specs=[pl.BlockSpec(memory_space=pltpu.VMEM)] * 3,
        out_specs=(pl.BlockSpec(memory_space=pl.ANY),) * 2,
        scratch_shapes=[
            pltpu.VMEM((2, B, B), F32),
            pltpu.VMEM((B, B), F32),
            pltpu.SemaphoreType.DMA((6,)),
        ],
        compiler_params=pltpu.CompilerParams(vmem_limit_bytes=32 * MIB),
    )(grad, stats_old, stale_roots)


def shards(acts, cotangent, example_of, stats_old, stale_roots):
    return block_step(*gather(acts, cotangent, example_of.reshape(1, B), stats_old, stale_roots))


def solution(mesh):
    return jax.shard_map(
        shards,
        mesh=mesh,
        in_specs=(
            P(("role", "fsdp"), "dp"),
            P("dp", ("role", "fsdp")),
            P("dp", None),
            P("dp", ("role", "fsdp"), None, None, None),
            P("dp", "fsdp", None, None, None),
        ),
        out_specs=(P("dp", ("role", "fsdp")), P("dp", ("role", "fsdp"), None, None, None)),
        check_vma=False,
    )
```

```python
import functools

import jax
import jax.numpy as jnp
from jax import lax
from jax.experimental import pallas as pl
from jax.experimental.pallas import tpu as pltpu
from jax.sharding import PartitionSpec as P

MESH = pl.DeviceIdType.MESH
F32 = jnp.float32
BF16 = jnp.bfloat16
B = 512
Q = 128
EXAMPLES = 128
MIB = 1 << 20


def contract(left, right, left_dim, right_dim):
    return lax.dot_general(
        left, right, (((left_dim,), (right_dim,)), ((), ())), preferred_element_type=F32
    )


class Names:
    def __init__(self):
        self.table = {}

    def __call__(self, *key):
        return self.table.setdefault(key, len(self.table))


COPIES = 96


def gather_kernel(
    acts_ref,
    cot_ref,
    ids_ref,
    stats_ref,
    stale_ref,
    grad_ref,
    stats_out,
    stale_out,
    acts_all,
    cot_all,
    ids_all,
    weights,
    local_sem,
    send_sem,
    recv_sem,
):
    role = lax.axis_index("role")
    fsdp = lax.axis_index("fsdp")
    dp = lax.axis_index("dp")
    z, core = fsdp // 2, fsdp % 2
    y, half = dp // 2, dp % 2
    number = Names()

    def device(role=role, z=z, core=core, y=y, half=half):
        return (role, z * 2 + core, y * 2 + half)

    across = device(half=1 - half)
    y_up, y_down = device(y=(y + 1) % 4), device(y=(y + 3) % 4)
    z_up, z_down = device(z=(z + 1) % 8), device(z=(z + 7) % 8)
    partner = device(role=1 - role)
    sibling = device(core=1 - core)
    row_peers = [(role, fsdp, (dp + step) % 8) for step in range(1, 8)]

    def acts_block(block_role, block_z, block_core):
        index = block_role * 16 + block_z * 2 + block_core
        return acts_all.at[index // 4, pl.ds(pl.multiple_of((index % 4) * Q, Q), Q)]

    def cot_part(block_y, block_half, quarter):
        return cot_all.at[block_y * 2 + block_half, pl.ds(quarter * Q, Q)]

    sent = []

    def copy_of(ref, key, target):
        index = number(*key)
        return pltpu.make_async_remote_copy(
            src_ref=ref,
            dst_ref=ref,
            send_sem=send_sem.at[index],
            recv_sem=recv_sem.at[index],
            device_id=target,
            device_id_type=MESH,
        )

    def send(ref, key, target):
        copy = copy_of(ref, key, target)
        copy.start()
        sent.append(copy)

    def arrived(ref, key):
        copy_of(ref, key, sibling).wait_recv()

    own_acts = acts_block(role, z, core)
    own_cot = cot_all.at[dp]
    local = [
        pltpu.make_async_copy(ids_ref, ids_all.at[dp], local_sem.at[0]),
        pltpu.make_async_copy(acts_ref, own_acts, local_sem.at[1]),
        pltpu.make_async_copy(cot_ref, own_cot, local_sem.at[2]),
    ]
    for copy in local:
        copy.start()

    barrier = pltpu.get_barrier_semaphore()
    others = [y_up, y_down, across] + [
        device(y=(y + 1) % 4, half=1 - half),
        device(y=(y + 3) % 4, half=1 - half),
        device(y=(y + 2) % 4),
        device(y=(y + 2) % 4, half=1 - half),
    ]
    everyone = others + [z_up, z_down, partner, sibling]
    for target in everyone:
        pl.semaphore_signal(barrier, inc=1, device_id=target, device_id_type=MESH)
    for copy in local:
        copy.wait()
    ahead = [
        pltpu.make_async_copy(stats_ref.at[0, 0], stats_out, local_sem.at[3]),
        pltpu.make_async_copy(stale_ref.at[0, 0], stale_out, local_sem.at[4]),
    ]
    for copy in ahead:
        copy.start()
    pl.semaphore_wait(barrier, len(everyone))

    for step, target in enumerate(row_peers, 1):
        send(ids_all.at[dp], ("ids", step), target)
    send(own_acts, ("partner",), partner)
    send(own_acts, ("up", 0, 1), z_up)
    send(own_acts, ("down", 0, 1), z_down)

    def own(quarter, direction):
        send(cot_part(y, half, quarter), ("y", direction, 0, quarter), y_up if direction else y_down)

    for pair in ((0, 3), (1, 2)):
        own(pair[0], 1)
        own(pair[1], 0)
        for quarter in pair:
            send(cot_part(y, half, quarter), ("x", 0, quarter), across)
    send(own_acts, ("sibling", 0, 0), sibling)

    for step in range(1, 8):
        arrived(ids_all.at[(dp + 8 - step) % 8], ("ids", step))

    def onehot(block):
        labels = lax.broadcasted_iota(jnp.int32, (EXAMPLES, B), 0)
        return jnp.where(ids_all[block] == labels, 1.0, 0.0)

    seen = lax.fori_loop(1, 8, lambda block, seen: seen + onehot(block), onehot(0))
    inverse = jnp.broadcast_to(1.0 / jnp.sum(seen, axis=1, keepdims=True), (EXAMPLES, Q))
    high = inverse.astype(BF16)
    rest = inverse - high.astype(F32)
    middle = rest.astype(BF16)
    low = (rest - middle.astype(F32)).astype(BF16)
    split = jnp.concatenate([high, middle, low], axis=1)

    def weigh(block, carry):
        spread = contract(onehot(block).astype(BF16), split, 0, 0)
        weights[block] = (spread[:, :Q] + spread[:, Q : 2 * Q]) + spread[:, 2 * Q :]
        return carry

    def step_acts(stream, hop):
        stream_role = role if stream == 0 else 1 - role
        for key, sign, target in (("up", -1, z_up), ("down", 1, z_down)):
            if hop == 4 and stream != (0 if key == "up" else 1):
                continue
            block = acts_block(stream_role, (z + 8 + sign * hop) % 8, core)
            arrived(block, (key, stream, hop))
            if hop < 3 or (hop == 3 and stream == (0 if key == "up" else 1)):
                send(block, (key, stream, hop + 1), target)
            send(block, ("sibling", stream, (8 + sign * hop) % 8), sibling)

    def from_sibling(offset):
        for stream in range(2):
            stream_role = role if stream == 0 else 1 - role
            arrived(acts_block(stream_role, (z + offset) % 8, 1 - core), ("sibling", stream, offset))

    up_y, down_y, far_y = (y + 1) % 4, (y + 3) % 4, (y + 2) % 4

    def pass_on(first, second):
        part = cot_part(down_y, half, first)
        arrived(part, ("y", 1, 0, first))
        send(part, ("y", 1, 1, first), y_up)
        part = cot_part(up_y, half, second)
        arrived(part, ("y", 0, 0, second))
        send(part, ("y", 0, 1, second), y_down)

    far = [copy_of(cot_part(far_y, half, quarter), ("x", 1, quarter), across) for quarter in (0, 3, 1, 2)]

    def send_far(*which):
        def start():
            for index in which:
                far[index].start()

        return start

    def far_arrived(*quarters):
        for quarter in quarters:
            arrived(cot_part(far_y, half, quarter), ("y", 1 if quarter < 2 else 0, 1, quarter))

    pass_on(0, 3)
    block = acts_block(1 - role, z, core)
    arrived(block, ("partner",))
    send(block, ("up", 1, 1), z_up)
    send(block, ("down", 1, 1), z_down)
    send(block, ("sibling", 1, 0), sibling)
    step_acts(0, 1)
    pass_on(1, 2)
    for quarter in (2, 3):
        own(quarter, 1)
        own(3 - quarter, 0)

    step_acts(1, 1)
    far_arrived(0, 3)
    send_far(0, 1)()
    far_arrived(1, 2)
    send_far(2, 3)()
    step_acts(0, 2)
    for quarter in (0, 3, 1):
        part = cot_part(y, 1 - half, quarter)
        arrived(part, ("x", 0, quarter))
        send(part, ("y", 1, 2, quarter), y_up)
        send(part, ("y", 0, 2, quarter), y_down)
    arrived(cot_part(y, 1 - half, 2), ("x", 0, 2))
    arrived(cot_part(down_y, half, 2), ("y", 1, 0, 2))
    send(
        cot_part(y, 1 - half, 2),
        ("y", 1, 2, 2),
        y_up,
    )
    send(
        cot_part(y, 1 - half, 2),
        ("y", 0, 2, 2),
        y_down,
    )
    step_acts(1, 2)
    lax.fori_loop(0, 8, weigh, 0)
    grad_ref[...] = jnp.zeros((B, B), F32)
    step_acts(0, 3)

    arrived(cot_part(down_y, half, 3), ("y", 1, 0, 3))
    for quarter in (0, 1):
        arrived(cot_part(up_y, half, quarter), ("y", 0, 0, quarter))

    def scaled(block, rows):
        weight = weights[block, rows]
        return jnp.concatenate(
            [
                (cot_all[block, rows, pl.ds(lane, Q)].astype(F32) * weight).astype(BF16)
                for lane in range(0, B, Q)
            ],
            axis=1,
        )

    def pair_distance(block):
        return (block % 4 * 2 + 8 - z // 2 * 2) % 8

    def stage(block):
        begin = pair_distance(block)
        odd = z % 2
        return jnp.where(begin == 4, 2, jnp.where(begin == 2 + 4 * odd, 1, 0))

    def early(want):
        def one(index, carry):
            block = (y + index % 4) % 4 * 2 + (half + index // 4) % 2

            @pl.when(stage(block) == want)
            def _():
                grad_ref[...] += contract(acts_all[block], scaled(block, pl.ds(0, B)), 0, 0)

            return carry

        lax.fori_loop(0, 5, one, 0)

    def outer(last):
        def one(index, carry):
            block = (y + 1 + index) % 4 * 2 + 1 - half
            rows = [pl.ds(0, Q), pl.ds(3 * Q, Q)]

            @pl.when((stage(block) == 2) == last)
            def _():
                grad_ref[...] += contract(
                    jnp.concatenate([acts_all[block, part] for part in rows], axis=0),
                    jnp.concatenate([scaled(block, part) for part in rows], axis=0),
                    0,
                    0,
                )

            return carry

        lax.fori_loop(0, 3, one, 0)

    def wave_arrived(quarter):
        arrived(cot_part(down_y, 1 - half, quarter), ("y", 1, 2, quarter))
        arrived(cot_part(up_y, 1 - half, quarter), ("y", 0, 2, quarter))
        arrived(cot_part(far_y, 1 - half, quarter), ("x", 1, quarter))

    late = [block_y * 2 + 1 - half for block_y in (up_y, far_y, down_y)]
    for offset in (0, 1, 7, 2, 6):
        from_sibling(offset)
    early(0)
    step_acts(1, 3)
    from_sibling(3)
    from_sibling(5)
    early(1)
    wave_arrived(0)
    wave_arrived(3)
    outer(False)
    step_acts(0, 4)
    step_acts(1, 4)
    from_sibling(4)
    early(2)
    outer(True)
    for quarter in (1, 2):
        wave_arrived(quarter)
        rows = pl.ds(quarter * Q, Q)
        grad_ref[...] += contract(
            jnp.concatenate([acts_all[block, rows] for block in late], axis=0),
            jnp.concatenate([scaled(block, rows) for block in late], axis=0),
            0,
            0,
        )

    for copy in ahead:
        copy.wait()
    for copy in sent + far:
        copy.wait_send()
    assert len(number.table) <= COPIES


def gather(*operands):
    operands = [pltpu.with_memory_space_constraint(operand, pltpu.HBM) for operand in operands]
    return pl.pallas_call(
        gather_kernel,
        out_shape=(
            pltpu.VMEM((B, B), F32),
            pltpu.VMEM((2, B, B), F32),
            pltpu.VMEM((2, B, B), F32),
        ),
        in_specs=[pl.BlockSpec(memory_space=pltpu.HBM)] * 5,
        out_specs=(pl.BlockSpec(memory_space=pltpu.VMEM),) * 3,
        scratch_shapes=[
            pltpu.VMEM((8, B, B), BF16),
            pltpu.VMEM((8, B, B), BF16),
            pltpu.VMEM((8, 1, B), jnp.int32),
            pltpu.VMEM((8, B, Q), F32),
            pltpu.SemaphoreType.DMA((5,)),
            pltpu.SemaphoreType.DMA((COPIES,)),
            pltpu.SemaphoreType.DMA((COPIES,)),
        ],
        compiler_params=pltpu.CompilerParams(
            collective_id=0, has_side_effects=True, vmem_limit_bytes=24 * MIB
        ),
    )(*operands)


def parts_of(matrix):
    high = matrix.astype(BF16)
    return high, (matrix - high.astype(F32)).astype(BF16)


def precise(left, right, left_dim, right_dim):
    (left_high, left_low), (right_high, right_low) = left, right
    return contract(
        jnp.concatenate([left_high, left_low, left_high], axis=left_dim),
        jnp.concatenate([right_high, right_high, right_low], axis=right_dim),
        left_dim,
        right_dim,
    )


def rough(left, right):
    return contract(left.astype(BF16), right.astype(BF16), 1, 0)


def total(matrix):
    return jnp.sum(jnp.sum(matrix, axis=0, keepdims=True), axis=1, keepdims=True)


def block_kernel(grad, stats, stale, update_ref, new_ref, fresh, update, ratio, store_sem):
    role = lax.axis_index("role")
    stores = [
        pltpu.make_async_copy(fresh.at[0], new_ref.at[0, 0, 0], store_sem.at[0]),
        pltpu.make_async_copy(fresh.at[1], new_ref.at[0, 0, 1], store_sem.at[1]),
    ]
    rounded = grad[...].astype(BF16)
    for side in range(2):
        gram = contract(rounded, rounded, 1 - side, 1 - side)
        fresh[side] = 0.9 * stats[side] + (1.0 - 0.9) * gram
        stores[side].start()
    grad_size = jnp.sqrt(total(grad[...] * grad[...]) * (1.0 / (B * B)))

    def finish(product, scale):
        update[...] = product
        square = total(product * product) * (1.0 / (B * B))
        ratio[...] = grad_size * scale / jnp.sqrt(square * (scale * scale) + 1e-06)

    @pl.when(role == 0)
    def _():
        inner = precise(parts_of(stale[0]), parts_of(grad[...]), 1, 0)
        finish(precise(parts_of(inner), parts_of(stale[1]), 1, 0), jnp.ones((1, 1), F32))

    @pl.when(role == 1)
    def _():
        sides = range(2)
        a = [fresh[side].astype(BF16) for side in sides]
        square = [total(fresh[side] * fresh[side]) for side in sides]
        r = [lax.rsqrt(square[side]) for side in sides]
        u = [
            ((r[side] * r[side]) * rough(a[side], a[side]) - (10.0 * r[side]) * fresh[side]).astype(BF16)
            for side in sides
        ]
        w = [50.0 * u[side].astype(F32) + rough(u[side], u[side]) for side in sides]
        n = [
            (r[side] * (1.0 / 256)) * (625.0 * fresh[side] + rough(a[side], w[side])) for side in sides
        ]
        n2 = [rough(n[side], n[side]) for side in sides]
        n3 = [rough(n[side], n2[side]) for side in sides]
        n4 = [250.0 * n[side] - 25.0 * n2[side] + n3[side] for side in sides]
        g = [
            3125.0 * n2[side] - (1280.0 + 3125.0) * n[side] - 1250.0 * n3[side] + rough(n3[side], n4[side])
            for side in sides
        ]
        apart = [
            1.25 * g[side] - r[side] * (1600.0 * fresh[side] + 0.25 * rough(a[side], g[side])) for side in sides
        ]
        scale = [lax.rsqrt(jnp.sqrt(jnp.sqrt(value))) for value in square]
        inner = 8000.0 * grad[...] + rough(apart[0], grad[...])
        product = 8000.0 * inner + rough(inner, apart[1])
        finish(product, scale[0] * scale[1] * (1.0 / (4096.0 * 4096.0)))

    for part in range(4):
        rows = pl.ds(part * Q, Q)
        update[rows] = update[rows] * ratio[...]
        copy = pltpu.make_async_copy(update.at[rows], update_ref.at[rows], store_sem.at[2 + part])
        copy.start()
        stores.append(copy)
    for copy in stores:
        copy.wait()


def block_step(grad, stats_old, stale_roots):
    return pl.pallas_call(
        block_kernel,
        out_shape=(
            jax.ShapeDtypeStruct((B, B), F32),
            jax.ShapeDtypeStruct((1, 1, 2, B, B), F32),
        ),
        in_specs=[pl.BlockSpec(memory_space=pltpu.VMEM)] * 3,
        out_specs=(pl.BlockSpec(memory_space=pl.ANY),) * 2,
        scratch_shapes=[
            pltpu.VMEM((2, B, B), F32),
            pltpu.VMEM((B, B), F32),
            pltpu.VMEM((1, 1), F32),
            pltpu.SemaphoreType.DMA((6,)),
        ],
        compiler_params=pltpu.CompilerParams(vmem_limit_bytes=32 * MIB),
    )(grad, stats_old, stale_roots)


def shards(acts, cotangent, example_of, stats_old, stale_roots):
    return block_step(*gather(acts, cotangent, example_of.reshape(1, B), stats_old, stale_roots))


def solution(mesh):
    return jax.shard_map(
        shards,
        mesh=mesh,
        in_specs=(
            P(("role", "fsdp"), "dp"),
            P("dp", ("role", "fsdp")),
            P("dp", None),
            P("dp", ("role", "fsdp"), None, None, None),
            P("dp", "fsdp", None, None, None),
        ),
        out_specs=(P("dp", ("role", "fsdp")), P("dp", ("role", "fsdp"), None, None, None)),
        check_vma=False,
    )
```

```python
import functools

import jax
import jax.numpy as jnp
from jax import lax
from jax.experimental import pallas as pl
from jax.experimental.pallas import tpu as pltpu
from jax.sharding import PartitionSpec as P

MESH = pl.DeviceIdType.MESH
F32 = jnp.float32
BF16 = jnp.bfloat16
B = 512
Q = 128
EXAMPLES = 128
REST = 48
MIB = 1 << 20


def contract(left, right, left_dim, right_dim):
    return lax.dot_general(
        left, right, (((left_dim,), (right_dim,)), ((), ())), preferred_element_type=F32
    )


class Names:
    def __init__(self):
        self.table = {}

    def __call__(self, *key):
        return self.table.setdefault(key, len(self.table))


COPIES = 96


def gather_kernel(
    acts_ref,
    cot_ref,
    ids_ref,
    stats_ref,
    stale_ref,
    grad_ref,
    stats_out,
    stale_out,
    acts_all,
    cot_all,
    ids_all,
    weights,
    local_sem,
    send_sem,
    recv_sem,
):
    role = lax.axis_index("role")
    fsdp = lax.axis_index("fsdp")
    dp = lax.axis_index("dp")
    z, core = fsdp // 2, fsdp % 2
    y, half = dp // 2, dp % 2
    number = Names()

    def device(role=role, z=z, core=core, y=y, half=half):
        return (role, z * 2 + core, y * 2 + half)

    across = device(half=1 - half)
    y_up, y_down = device(y=(y + 1) % 4), device(y=(y + 3) % 4)
    z_up, z_down = device(z=(z + 1) % 8), device(z=(z + 7) % 8)
    partner = device(role=1 - role)
    sibling = device(core=1 - core)
    row_peers = [(role, fsdp, (dp + step) % 8) for step in range(1, 8)]

    def acts_block(block_role, block_z, block_core):
        index = block_role * 16 + block_z * 2 + block_core
        return acts_all.at[index // 4, pl.ds(pl.multiple_of((index % 4) * Q, Q), Q)]

    def cot_part(block_y, block_half, quarter):
        return cot_all.at[block_y * 2 + block_half, pl.ds(quarter * Q, Q)]

    def head_of(block_y, block_half):
        return cot_all.at[block_y * 2 + block_half, pl.ds(2 * Q, Q - REST)]

    def rest_of(block_y, block_half):
        return cot_all.at[block_y * 2 + block_half, pl.ds(3 * Q - REST, REST)]

    sent = []

    def copy_of(ref, key, target):
        index = number(*key)
        return pltpu.make_async_remote_copy(
            src_ref=ref,
            dst_ref=ref,
            send_sem=send_sem.at[index],
            recv_sem=recv_sem.at[index],
            device_id=target,
            device_id_type=MESH,
        )

    def send(ref, key, target):
        copy = copy_of(ref, key, target)
        copy.start()
        sent.append(copy)

    def arrived(ref, key):
        copy_of(ref, key, sibling).wait_recv()

    own_acts = acts_block(role, z, core)
    own_cot = cot_all.at[dp]
    local = [
        pltpu.make_async_copy(ids_ref, ids_all.at[dp], local_sem.at[0]),
        pltpu.make_async_copy(acts_ref, own_acts, local_sem.at[1]),
        pltpu.make_async_copy(cot_ref, own_cot, local_sem.at[2]),
    ]
    for copy in local:
        copy.start()

    barrier = pltpu.get_barrier_semaphore()
    others = [y_up, y_down, across] + [
        device(y=(y + 1) % 4, half=1 - half),
        device(y=(y + 3) % 4, half=1 - half),
        device(y=(y + 2) % 4),
        device(y=(y + 2) % 4, half=1 - half),
    ]
    everyone = others + [z_up, z_down, partner, sibling]
    for target in everyone:
        pl.semaphore_signal(barrier, inc=1, device_id=target, device_id_type=MESH)
    for copy in local:
        copy.wait()
    ahead = [
        pltpu.make_async_copy(stats_ref.at[0, 0], stats_out, local_sem.at[3]),
        pltpu.make_async_copy(stale_ref.at[0, 0], stale_out, local_sem.at[4]),
    ]
    for copy in ahead:
        copy.start()
    pl.semaphore_wait(barrier, len(everyone))

    for step, target in enumerate(row_peers, 1):
        send(ids_all.at[dp], ("ids", step), target)
    send(own_acts, ("partner",), partner)
    send(own_acts, ("up", 0, 1), z_up)
    send(own_acts, ("down", 0, 1), z_down)

    def own(quarter, direction):
        send(cot_part(y, half, quarter), ("y", direction, 0, quarter), y_up if direction else y_down)

    for pair in ((0, 3), (1, 2)):
        own(pair[0], 1)
        own(pair[1], 0)
        for quarter in pair:
            send(cot_part(y, half, quarter), ("x", 0, quarter), across)
    send(own_acts, ("sibling", 0, 0), sibling)

    for step in range(1, 8):
        arrived(ids_all.at[(dp + 8 - step) % 8], ("ids", step))

    def onehot(block):
        labels = lax.broadcasted_iota(jnp.int32, (EXAMPLES, B), 0)
        return jnp.where(ids_all[block] == labels, 1.0, 0.0)

    seen = lax.fori_loop(1, 8, lambda block, seen: seen + onehot(block), onehot(0))
    inverse = jnp.broadcast_to(1.0 / jnp.sum(seen, axis=1, keepdims=True), (EXAMPLES, Q))
    high = inverse.astype(BF16)
    rest = inverse - high.astype(F32)
    middle = rest.astype(BF16)
    low = (rest - middle.astype(F32)).astype(BF16)
    split = jnp.concatenate([high, middle, low], axis=1)

    def weigh(block, carry):
        spread = contract(onehot(block).astype(BF16), split, 0, 0)
        weights[block] = (spread[:, :Q] + spread[:, Q : 2 * Q]) + spread[:, 2 * Q :]
        return carry

    def step_acts(stream, hop):
        stream_role = role if stream == 0 else 1 - role
        for key, sign, target in (("up", -1, z_up), ("down", 1, z_down)):
            if hop == 4 and stream != (0 if key == "up" else 1):
                continue
            block = acts_block(stream_role, (z + 8 + sign * hop) % 8, core)
            arrived(block, (key, stream, hop))
            if hop < 3 or (hop == 3 and stream == (0 if key == "up" else 1)):
                send(block, (key, stream, hop + 1), target)
            send(block, ("sibling", stream, (8 + sign * hop) % 8), sibling)

    def from_sibling(offset):
        for stream in range(2):
            stream_role = role if stream == 0 else 1 - role
            arrived(acts_block(stream_role, (z + offset) % 8, 1 - core), ("sibling", stream, offset))

    up_y, down_y, far_y = (y + 1) % 4, (y + 3) % 4, (y + 2) % 4

    def pass_on(first, second):
        part = cot_part(down_y, half, first)
        arrived(part, ("y", 1, 0, first))
        send(part, ("y", 1, 1, first), y_up)
        part = cot_part(up_y, half, second)
        arrived(part, ("y", 0, 0, second))
        send(part, ("y", 0, 1, second), y_down)

    far = [copy_of(cot_part(far_y, half, quarter), ("x", 1, quarter), across) for quarter in (0, 3, 1, 2)]

    def send_far(*which):
        def start():
            for index in which:
                far[index].start()

        return start

    def far_arrived(*quarters):
        for quarter in quarters:
            arrived(cot_part(far_y, half, quarter), ("y", 1 if quarter < 2 else 0, 1, quarter))

    pass_on(0, 3)
    block = acts_block(1 - role, z, core)
    arrived(block, ("partner",))
    send(block, ("up", 1, 1), z_up)
    send(block, ("down", 1, 1), z_down)
    send(block, ("sibling", 1, 0), sibling)
    step_acts(0, 1)
    pass_on(1, 2)
    for quarter in (2, 3):
        own(quarter, 1)
        own(3 - quarter, 0)

    step_acts(1, 1)
    far_arrived(0, 3)
    send_far(0, 1)()
    far_arrived(1, 2)
    send_far(2, 3)()
    step_acts(0, 2)
    for quarter in (0, 3, 1):
        part = cot_part(y, 1 - half, quarter)
        arrived(part, ("x", 0, quarter))
        send(part, ("y", 1, 2, quarter), y_up)
        send(part, ("y", 0, 2, quarter), y_down)
    arrived(cot_part(y, 1 - half, 2), ("x", 0, 2))
    arrived(cot_part(down_y, half, 2), ("y", 1, 0, 2))
    part = head_of(y, 1 - half)
    send(part, ("y", 1, 2, 2), y_up)
    send(part, ("y", 0, 2, 2), y_down)
    send(rest_of(down_y, half), ("x", 2, 0), across)
    send(rest_of(up_y, half), ("x", 2, 1), across)
    step_acts(1, 2)
    lax.fori_loop(0, 8, weigh, 0)
    grad_ref[...] = jnp.zeros((B, B), F32)
    step_acts(0, 3)

    arrived(cot_part(down_y, half, 3), ("y", 1, 0, 3))
    for quarter in (0, 1):
        arrived(cot_part(up_y, half, quarter), ("y", 0, 0, quarter))

    def scaled(block, rows):
        weight = weights[block, rows]
        return jnp.concatenate(
            [
                (cot_all[block, rows, pl.ds(lane, Q)].astype(F32) * weight).astype(BF16)
                for lane in range(0, B, Q)
            ],
            axis=1,
        )

    def pair_distance(block):
        return (block % 4 * 2 + 8 - z // 2 * 2) % 8

    def stage(block):
        begin = pair_distance(block)
        odd = z % 2
        return jnp.where(begin == 4, 2, jnp.where(begin == 2 + 4 * odd, 1, 0))

    def early(want):
        def one(index, carry):
            block = (y + index % 4) % 4 * 2 + (half + index // 4) % 2

            @pl.when(stage(block) == want)
            def _():
                grad_ref[...] += contract(acts_all[block], scaled(block, pl.ds(0, B)), 0, 0)

            return carry

        lax.fori_loop(0, 5, one, 0)

    def outer(last):
        def one(index, carry):
            block = (y + 1 + index) % 4 * 2 + 1 - half
            rows = [pl.ds(0, Q), pl.ds(3 * Q, Q)]

            @pl.when((stage(block) == 2) == last)
            def _():
                grad_ref[...] += contract(
                    jnp.concatenate([acts_all[block, part] for part in rows], axis=0),
                    jnp.concatenate([scaled(block, part) for part in rows], axis=0),
                    0,
                    0,
                )

            return carry

        lax.fori_loop(0, 3, one, 0)

    def wave_arrived(quarter):
        part_of = head_of if quarter == 2 else functools.partial(cot_part, quarter=quarter)
        arrived(part_of(down_y, 1 - half), ("y", 1, 2, quarter))
        arrived(part_of(up_y, 1 - half), ("y", 0, 2, quarter))
        if quarter == 2:
            arrived(rest_of(down_y, 1 - half), ("x", 2, 0))
            arrived(rest_of(up_y, 1 - half), ("x", 2, 1))
        arrived(cot_part(far_y, 1 - half, quarter), ("x", 1, quarter))

    late = [block_y * 2 + 1 - half for block_y in (up_y, far_y, down_y)]
    for offset in (0, 1, 7, 2, 6):
        from_sibling(offset)
    early(0)
    step_acts(1, 3)
    from_sibling(3)
    from_sibling(5)
    early(1)
    wave_arrived(0)
    wave_arrived(3)
    outer(False)
    step_acts(0, 4)
    step_acts(1, 4)
    from_sibling(4)
    early(2)
    outer(True)
    for quarter in (1, 2):
        wave_arrived(quarter)
        rows = pl.ds(quarter * Q, Q)
        grad_ref[...] += contract(
            jnp.concatenate([acts_all[block, rows] for block in late], axis=0),
            jnp.concatenate([scaled(block, rows) for block in late], axis=0),
            0,
            0,
        )

    for copy in ahead:
        copy.wait()
    for copy in sent + far:
        copy.wait_send()
    assert len(number.table) <= COPIES


def gather(*operands):
    operands = [pltpu.with_memory_space_constraint(operand, pltpu.HBM) for operand in operands]
    return pl.pallas_call(
        gather_kernel,
        out_shape=(
            pltpu.VMEM((B, B), F32),
            pltpu.VMEM((2, B, B), F32),
            pltpu.VMEM((2, B, B), F32),
        ),
        in_specs=[pl.BlockSpec(memory_space=pltpu.HBM)] * 5,
        out_specs=(pl.BlockSpec(memory_space=pltpu.VMEM),) * 3,
        scratch_shapes=[
            pltpu.VMEM((8, B, B), BF16),
            pltpu.VMEM((8, B, B), BF16),
            pltpu.VMEM((8, 1, B), jnp.int32),
            pltpu.VMEM((8, B, Q), F32),
            pltpu.SemaphoreType.DMA((5,)),
            pltpu.SemaphoreType.DMA((COPIES,)),
            pltpu.SemaphoreType.DMA((COPIES,)),
        ],
        compiler_params=pltpu.CompilerParams(
            collective_id=0, has_side_effects=True, vmem_limit_bytes=24 * MIB
        ),
    )(*operands)


def parts_of(matrix):
    high = matrix.astype(BF16)
    return high, (matrix - high.astype(F32)).astype(BF16)


def precise(left, right, left_dim, right_dim):
    (left_high, left_low), (right_high, right_low) = left, right
    return contract(
        jnp.concatenate([left_high, left_low, left_high], axis=left_dim),
        jnp.concatenate([right_high, right_high, right_low], axis=right_dim),
        left_dim,
        right_dim,
    )


def rough(left, right):
    return contract(left.astype(BF16), right.astype(BF16), 1, 0)


def total(matrix):
    return jnp.sum(jnp.sum(matrix, axis=0, keepdims=True), axis=1, keepdims=True)


def block_kernel(grad, stats, stale, update_ref, new_ref, fresh, update, ratio, store_sem):
    role = lax.axis_index("role")
    stores = [
        pltpu.make_async_copy(fresh.at[0], new_ref.at[0, 0, 0], store_sem.at[0]),
        pltpu.make_async_copy(fresh.at[1], new_ref.at[0, 0, 1], store_sem.at[1]),
    ]
    rounded = grad[...].astype(BF16)
    for side in range(2):
        gram = contract(rounded, rounded, 1 - side, 1 - side)
        fresh[side] = 0.9 * stats[side] + (1.0 - 0.9) * gram
        stores[side].start()
    grad_size = jnp.sqrt(total(grad[...] * grad[...]) * (1.0 / (B * B)))

    def finish(product, scale):
        update[...] = product
        square = total(product * product) * (1.0 / (B * B))
        ratio[...] = grad_size * scale / jnp.sqrt(square * (scale * scale) + 1e-06)

    @pl.when(role == 0)
    def _():
        inner = precise(parts_of(stale[0]), parts_of(grad[...]), 1, 0)
        finish(precise(parts_of(inner), parts_of(stale[1]), 1, 0), jnp.ones((1, 1), F32))

    @pl.when(role == 1)
    def _():
        sides = range(2)
        a = [fresh[side].astype(BF16) for side in sides]
        square = [total(fresh[side] * fresh[side]) for side in sides]
        r = [lax.rsqrt(square[side]) for side in sides]
        u = [
            ((r[side] * r[side]) * rough(a[side], a[side]) - (10.0 * r[side]) * fresh[side]).astype(BF16)
            for side in sides
        ]
        w = [50.0 * u[side].astype(F32) + rough(u[side], u[side]) for side in sides]
        n = [
            (r[side] * (1.0 / 256)) * (625.0 * fresh[side] + rough(a[side], w[side])) for side in sides
        ]
        n2 = [rough(n[side], n[side]) for side in sides]
        n3 = [rough(n[side], n2[side]) for side in sides]
        n4 = [250.0 * n[side] - 25.0 * n2[side] + n3[side] for side in sides]
        g = [
            3125.0 * n2[side] - (1280.0 + 3125.0) * n[side] - 1250.0 * n3[side] + rough(n3[side], n4[side])
            for side in sides
        ]
        apart = [
            1.25 * g[side] - r[side] * (1600.0 * fresh[side] + 0.25 * rough(a[side], g[side])) for side in sides
        ]
        scale = [lax.rsqrt(jnp.sqrt(jnp.sqrt(value))) for value in square]
        inner = 8000.0 * grad[...] + rough(apart[0], grad[...])
        product = 8000.0 * inner + rough(inner, apart[1])
        finish(product, scale[0] * scale[1] * (1.0 / (4096.0 * 4096.0)))

    for part in range(4):
        rows = pl.ds(part * Q, Q)
        update[rows] = update[rows] * ratio[...]
        copy = pltpu.make_async_copy(update.at[rows], update_ref.at[rows], store_sem.at[2 + part])
        copy.start()
        stores.append(copy)
    for copy in stores:
        copy.wait()


def block_step(grad, stats_old, stale_roots):
    return pl.pallas_call(
        block_kernel,
        out_shape=(
            jax.ShapeDtypeStruct((B, B), F32),
            jax.ShapeDtypeStruct((1, 1, 2, B, B), F32),
        ),
        in_specs=[pl.BlockSpec(memory_space=pltpu.VMEM)] * 3,
        out_specs=(pl.BlockSpec(memory_space=pl.ANY),) * 2,
        scratch_shapes=[
            pltpu.VMEM((2, B, B), F32),
            pltpu.VMEM((B, B), F32),
            pltpu.VMEM((1, 1), F32),
            pltpu.SemaphoreType.DMA((6,)),
        ],
        compiler_params=pltpu.CompilerParams(vmem_limit_bytes=32 * MIB),
    )(grad, stats_old, stale_roots)


def shards(acts, cotangent, example_of, stats_old, stale_roots):
    return block_step(*gather(acts, cotangent, example_of.reshape(1, B), stats_old, stale_roots))


def solution(mesh):
    return jax.shard_map(
        shards,
        mesh=mesh,
        in_specs=(
            P(("role", "fsdp"), "dp"),
            P("dp", ("role", "fsdp")),
            P("dp", None),
            P("dp", ("role", "fsdp"), None, None, None),
            P("dp", "fsdp", None, None, None),
        ),
        out_specs=(P("dp", ("role", "fsdp")), P("dp", ("role", "fsdp"), None, None, None)),
        check_vma=False,
    )
```

```python
import functools

import jax
import jax.numpy as jnp
from jax import lax
from jax.experimental import pallas as pl
from jax.experimental.pallas import tpu as pltpu
from jax.sharding import PartitionSpec as P

MESH = pl.DeviceIdType.MESH
F32 = jnp.float32
BF16 = jnp.bfloat16
B = 512
Q = 128
EXAMPLES = 128
REST = 48
MIB = 1 << 20


def contract(left, right, left_dim, right_dim):
    return lax.dot_general(
        left, right, (((left_dim,), (right_dim,)), ((), ())), preferred_element_type=F32
    )


class Names:
    def __init__(self):
        self.table = {}

    def __call__(self, *key):
        return self.table.setdefault(key, len(self.table))


COPIES = 96


def gather_kernel(
    acts_ref,
    cot_ref,
    ids_ref,
    stats_ref,
    stale_ref,
    grad_ref,
    stats_out,
    stale_out,
    acts_all,
    cot_all,
    ids_all,
    weights,
    local_sem,
    send_sem,
    recv_sem,
):
    role = lax.axis_index("role")
    fsdp = lax.axis_index("fsdp")
    dp = lax.axis_index("dp")
    z, core = fsdp // 2, fsdp % 2
    y, half = dp // 2, dp % 2
    number = Names()

    def device(role=role, z=z, core=core, y=y, half=half):
        return (role, z * 2 + core, y * 2 + half)

    across = device(half=1 - half)
    y_up, y_down = device(y=(y + 1) % 4), device(y=(y + 3) % 4)
    z_up, z_down = device(z=(z + 1) % 8), device(z=(z + 7) % 8)
    partner = device(role=1 - role)
    sibling = device(core=1 - core)
    row_peers = [(role, fsdp, (dp + step) % 8) for step in range(1, 8)]

    def acts_block(block_role, block_z, block_core):
        index = block_role * 16 + block_z * 2 + block_core
        return acts_all.at[index // 4, pl.ds(pl.multiple_of((index % 4) * Q, Q), Q)]

    def cot_part(block_y, block_half, quarter):
        return cot_all.at[block_y * 2 + block_half, pl.ds(quarter * Q, Q)]

    def head_of(block_y, block_half):
        return cot_all.at[block_y * 2 + block_half, pl.ds(2 * Q, Q - REST)]

    def rest_of(block_y, block_half):
        return cot_all.at[block_y * 2 + block_half, pl.ds(3 * Q - REST, REST)]

    sent = []

    def copy_of(ref, key, target):
        index = number(*key)
        return pltpu.make_async_remote_copy(
            src_ref=ref,
            dst_ref=ref,
            send_sem=send_sem.at[index],
            recv_sem=recv_sem.at[index],
            device_id=target,
            device_id_type=MESH,
        )

    def send(ref, key, target):
        copy = copy_of(ref, key, target)
        copy.start()
        sent.append(copy)

    def arrived(ref, key):
        copy_of(ref, key, sibling).wait_recv()

    own_acts = acts_block(role, z, core)
    own_cot = cot_all.at[dp]
    local = [
        pltpu.make_async_copy(ids_ref, ids_all.at[dp], local_sem.at[0]),
        pltpu.make_async_copy(acts_ref, own_acts, local_sem.at[1]),
        pltpu.make_async_copy(cot_ref, own_cot, local_sem.at[2]),
    ]
    for copy in local:
        copy.start()

    barrier = pltpu.get_barrier_semaphore()
    others = [y_up, y_down, across] + [
        device(y=(y + 1) % 4, half=1 - half),
        device(y=(y + 3) % 4, half=1 - half),
        device(y=(y + 2) % 4),
        device(y=(y + 2) % 4, half=1 - half),
    ]
    everyone = others + [z_up, z_down, partner, sibling]
    for target in everyone:
        pl.semaphore_signal(barrier, inc=1, device_id=target, device_id_type=MESH)
    for copy in local:
        copy.wait()
    ahead = [
        pltpu.make_async_copy(stats_ref.at[0, 0], stats_out, local_sem.at[3]),
        pltpu.make_async_copy(stale_ref.at[0, 0], stale_out, local_sem.at[4]),
    ]
    for copy in ahead:
        copy.start()
    pl.semaphore_wait(barrier, len(everyone))

    for step, target in enumerate(row_peers, 1):
        send(ids_all.at[dp], ("ids", step), target)
    send(own_acts, ("partner",), partner)
    send(own_acts, ("up", 0, 1), z_up)
    send(own_acts, ("down", 0, 1), z_down)

    def own(quarter, direction):
        send(cot_part(y, half, quarter), ("y", direction, 0, quarter), y_up if direction else y_down)

    for pair in ((0, 3), (1, 2)):
        own(pair[0], 1)
        own(pair[1], 0)
        for quarter in pair:
            send(cot_part(y, half, quarter), ("x", 0, quarter), across)
    send(own_acts, ("sibling", 0, 0), sibling)

    for step in range(1, 8):
        arrived(ids_all.at[(dp + 8 - step) % 8], ("ids", step))

    def onehot(block):
        labels = lax.broadcasted_iota(jnp.int32, (EXAMPLES, B), 0)
        return jnp.where(ids_all[block] == labels, 1.0, 0.0)

    seen = lax.fori_loop(1, 8, lambda block, seen: seen + onehot(block), onehot(0))
    inverse = jnp.broadcast_to(1.0 / jnp.sum(seen, axis=1, keepdims=True), (EXAMPLES, Q))
    high = inverse.astype(BF16)
    rest = inverse - high.astype(F32)
    middle = rest.astype(BF16)
    low = (rest - middle.astype(F32)).astype(BF16)
    split = jnp.concatenate([high, middle, low], axis=1)

    def weigh(block, carry):
        spread = contract(onehot(block).astype(BF16), split, 0, 0)
        weights[block] = (spread[:, :Q] + spread[:, Q : 2 * Q]) + spread[:, 2 * Q :]
        return carry

    def step_acts(stream, hop):
        stream_role = role if stream == 0 else 1 - role
        for key, sign, target in (("up", -1, z_up), ("down", 1, z_down)):
            if hop == 4 and stream != (0 if key == "up" else 1):
                continue
            block = acts_block(stream_role, (z + 8 + sign * hop) % 8, core)
            arrived(block, (key, stream, hop))
            if hop < 3 or (hop == 3 and stream == (0 if key == "up" else 1)):
                send(block, (key, stream, hop + 1), target)
            send(block, ("sibling", stream, (8 + sign * hop) % 8), sibling)

    def from_sibling(offset):
        for stream in range(2):
            stream_role = role if stream == 0 else 1 - role
            arrived(acts_block(stream_role, (z + offset) % 8, 1 - core), ("sibling", stream, offset))

    up_y, down_y, far_y = (y + 1) % 4, (y + 3) % 4, (y + 2) % 4

    def pass_on(first, second):
        part = cot_part(down_y, half, first)
        arrived(part, ("y", 1, 0, first))
        send(part, ("y", 1, 1, first), y_up)
        part = cot_part(up_y, half, second)
        arrived(part, ("y", 0, 0, second))
        send(part, ("y", 0, 1, second), y_down)

    far = [copy_of(cot_part(far_y, half, quarter), ("x", 1, quarter), across) for quarter in (0, 3, 1, 2)]

    def send_far(*which):
        def start():
            for index in which:
                far[index].start()

        return start

    def far_arrived(*quarters):
        for quarter in quarters:
            arrived(cot_part(far_y, half, quarter), ("y", 1 if quarter < 2 else 0, 1, quarter))

    pass_on(0, 3)
    block = acts_block(1 - role, z, core)
    arrived(block, ("partner",))
    send(block, ("up", 1, 1), z_up)
    send(block, ("down", 1, 1), z_down)
    send(block, ("sibling", 1, 0), sibling)
    step_acts(0, 1)
    pass_on(1, 2)
    for quarter in (2, 3):
        own(quarter, 1)
        own(3 - quarter, 0)
    lax.fori_loop(0, 8, weigh, 0)

    step_acts(1, 1)
    far_arrived(0, 3)
    send_far(0, 1)()
    far_arrived(1, 2)
    send_far(2, 3)()
    step_acts(0, 2)
    for quarter in (0, 3, 1):
        part = cot_part(y, 1 - half, quarter)
        arrived(part, ("x", 0, quarter))
        send(part, ("y", 1, 2, quarter), y_up)
        send(part, ("y", 0, 2, quarter), y_down)
    arrived(cot_part(y, 1 - half, 2), ("x", 0, 2))
    arrived(cot_part(down_y, half, 2), ("y", 1, 0, 2))
    part = head_of(y, 1 - half)
    send(part, ("y", 1, 2, 2), y_up)
    send(part, ("y", 0, 2, 2), y_down)
    send(rest_of(down_y, half), ("x", 2, 0), across)
    send(rest_of(up_y, half), ("x", 2, 1), across)
    step_acts(1, 2)
    grad_ref[...] = jnp.zeros((B, B), F32)
    step_acts(0, 3)

    arrived(cot_part(down_y, half, 3), ("y", 1, 0, 3))
    for quarter in (0, 1):
        arrived(cot_part(up_y, half, quarter), ("y", 0, 0, quarter))

    def scaled(block, rows):
        weight = weights[block, rows]
        return jnp.concatenate(
            [
                (cot_all[block, rows, pl.ds(lane, Q)].astype(F32) * weight).astype(BF16)
                for lane in range(0, B, Q)
            ],
            axis=1,
        )

    def pair_distance(block):
        return (block % 4 * 2 + 8 - z // 2 * 2) % 8

    def stage(block):
        begin = pair_distance(block)
        odd = z % 2
        return jnp.where(begin == 4, 2, jnp.where(begin == 2 + 4 * odd, 1, 0))

    def early(want):
        def one(index, carry):
            block = (y + index % 4) % 4 * 2 + (half + index // 4) % 2

            @pl.when(stage(block) == want)
            def _():
                grad_ref[...] += contract(acts_all[block], scaled(block, pl.ds(0, B)), 0, 0)

            return carry

        lax.fori_loop(0, 5, one, 0)

    def outer(last):
        def one(index, carry):
            block = (y + 1 + index) % 4 * 2 + 1 - half
            rows = [pl.ds(0, Q), pl.ds(3 * Q, Q)]

            @pl.when((stage(block) == 2) == last)
            def _():
                grad_ref[...] += contract(
                    jnp.concatenate([acts_all[block, part] for part in rows], axis=0),
                    jnp.concatenate([scaled(block, part) for part in rows], axis=0),
                    0,
                    0,
                )

            return carry

        lax.fori_loop(0, 3, one, 0)

    def wave_arrived(quarter):
        part_of = head_of if quarter == 2 else functools.partial(cot_part, quarter=quarter)
        arrived(part_of(down_y, 1 - half), ("y", 1, 2, quarter))
        arrived(part_of(up_y, 1 - half), ("y", 0, 2, quarter))
        if quarter == 2:
            arrived(rest_of(down_y, 1 - half), ("x", 2, 0))
            arrived(rest_of(up_y, 1 - half), ("x", 2, 1))
        arrived(cot_part(far_y, 1 - half, quarter), ("x", 1, quarter))

    late = [block_y * 2 + 1 - half for block_y in (up_y, far_y, down_y)]
    for offset in (0, 1, 7, 2, 6):
        from_sibling(offset)
    early(0)
    step_acts(1, 3)
    from_sibling(3)
    from_sibling(5)
    early(1)
    step_acts(0, 4)
    step_acts(1, 4)
    wave_arrived(0)
    wave_arrived(3)
    outer(False)
    from_sibling(4)
    early(2)
    outer(True)
    for quarter in (1, 2):
        wave_arrived(quarter)
        rows = pl.ds(quarter * Q, Q)
        grad_ref[...] += contract(
            jnp.concatenate([acts_all[block, rows] for block in late], axis=0),
            jnp.concatenate([scaled(block, rows) for block in late], axis=0),
            0,
            0,
        )

    for copy in ahead:
        copy.wait()
    for copy in sent + far:
        copy.wait_send()
    assert len(number.table) <= COPIES


def gather(*operands):
    operands = [pltpu.with_memory_space_constraint(operand, pltpu.HBM) for operand in operands]
    return pl.pallas_call(
        gather_kernel,
        out_shape=(
            pltpu.VMEM((B, B), F32),
            pltpu.VMEM((2, B, B), F32),
            pltpu.VMEM((2, B, B), F32),
        ),
        in_specs=[pl.BlockSpec(memory_space=pltpu.HBM)] * 5,
        out_specs=(pl.BlockSpec(memory_space=pltpu.VMEM),) * 3,
        scratch_shapes=[
            pltpu.VMEM((8, B, B), BF16),
            pltpu.VMEM((8, B, B), BF16),
            pltpu.VMEM((8, 1, B), jnp.int32),
            pltpu.VMEM((8, B, Q), F32),
            pltpu.SemaphoreType.DMA((5,)),
            pltpu.SemaphoreType.DMA((COPIES,)),
            pltpu.SemaphoreType.DMA((COPIES,)),
        ],
        compiler_params=pltpu.CompilerParams(
            collective_id=0, has_side_effects=True, vmem_limit_bytes=24 * MIB
        ),
    )(*operands)


def parts_of(matrix):
    high = matrix.astype(BF16)
    return high, (matrix - high.astype(F32)).astype(BF16)


def precise(left, right, left_dim, right_dim):
    (left_high, left_low), (right_high, right_low) = left, right
    return contract(
        jnp.concatenate([left_high, left_low, left_high], axis=left_dim),
        jnp.concatenate([right_high, right_high, right_low], axis=right_dim),
        left_dim,
        right_dim,
    )


def rough(left, right):
    return contract(left.astype(BF16), right.astype(BF16), 1, 0)


def total(matrix):
    return jnp.sum(jnp.sum(matrix, axis=0, keepdims=True), axis=1, keepdims=True)


def block_kernel(grad, stats, stale, update_ref, new_ref, fresh, update, ratio, store_sem):
    role = lax.axis_index("role")
    stores = [
        pltpu.make_async_copy(fresh.at[0], new_ref.at[0, 0, 0], store_sem.at[0]),
        pltpu.make_async_copy(fresh.at[1], new_ref.at[0, 0, 1], store_sem.at[1]),
    ]
    rounded = grad[...].astype(BF16)
    for side in range(2):
        gram = contract(rounded, rounded, 1 - side, 1 - side)
        fresh[side] = 0.9 * stats[side] + (1.0 - 0.9) * gram
        stores[side].start()
    grad_size = jnp.sqrt(total(grad[...] * grad[...]) * (1.0 / (B * B)))

    def finish(product, scale):
        update[...] = product
        square = total(product * product) * (1.0 / (B * B))
        ratio[...] = grad_size * scale / jnp.sqrt(square * (scale * scale) + 1e-06)

    @pl.when(role == 0)
    def _():
        inner = precise(parts_of(stale[0]), parts_of(grad[...]), 1, 0)
        finish(precise(parts_of(inner), parts_of(stale[1]), 1, 0), jnp.ones((1, 1), F32))

    @pl.when(role == 1)
    def _():
        sides = range(2)
        a = [fresh[side].astype(BF16) for side in sides]
        square = [total(fresh[side] * fresh[side]) for side in sides]
        r = [lax.rsqrt(square[side]) for side in sides]
        u = [
            ((r[side] * r[side]) * rough(a[side], a[side]) - (10.0 * r[side]) * fresh[side]).astype(BF16)
            for side in sides
        ]
        w = [50.0 * u[side].astype(F32) + rough(u[side], u[side]) for side in sides]
        n = [
            (r[side] * (1.0 / 256)) * (625.0 * fresh[side] + rough(a[side], w[side])) for side in sides
        ]
        n2 = [rough(n[side], n[side]) for side in sides]
        n3 = [rough(n[side], n2[side]) for side in sides]
        n4 = [250.0 * n[side] - 25.0 * n2[side] + n3[side] for side in sides]
        g = [
            3125.0 * n2[side] - (1280.0 + 3125.0) * n[side] - 1250.0 * n3[side] + rough(n3[side], n4[side])
            for side in sides
        ]
        apart = [
            1.25 * g[side] - r[side] * (1600.0 * fresh[side] + 0.25 * rough(a[side], g[side])) for side in sides
        ]
        scale = [lax.rsqrt(jnp.sqrt(jnp.sqrt(value))) for value in square]
        inner = 8000.0 * grad[...] + rough(apart[0], grad[...])
        product = 8000.0 * inner + rough(inner, apart[1])
        finish(product, scale[0] * scale[1] * (1.0 / (4096.0 * 4096.0)))

    for part in range(4):
        rows = pl.ds(part * Q, Q)
        update[rows] = update[rows] * ratio[...]
        copy = pltpu.make_async_copy(update.at[rows], update_ref.at[rows], store_sem.at[2 + part])
        copy.start()
        stores.append(copy)
    for copy in stores:
        copy.wait()


def block_step(grad, stats_old, stale_roots):
    return pl.pallas_call(
        block_kernel,
        out_shape=(
            jax.ShapeDtypeStruct((B, B), F32),
            jax.ShapeDtypeStruct((1, 1, 2, B, B), F32),
        ),
        in_specs=[pl.BlockSpec(memory_space=pltpu.VMEM)] * 3,
        out_specs=(pl.BlockSpec(memory_space=pl.ANY),) * 2,
        scratch_shapes=[
            pltpu.VMEM((2, B, B), F32),
            pltpu.VMEM((B, B), F32),
            pltpu.VMEM((1, 1), F32),
            pltpu.SemaphoreType.DMA((6,)),
        ],
        compiler_params=pltpu.CompilerParams(vmem_limit_bytes=32 * MIB),
    )(grad, stats_old, stale_roots)


def shards(acts, cotangent, example_of, stats_old, stale_roots):
    return block_step(*gather(acts, cotangent, example_of.reshape(1, B), stats_old, stale_roots))


def solution(mesh):
    return jax.shard_map(
        shards,
        mesh=mesh,
        in_specs=(
            P(("role", "fsdp"), "dp"),
            P("dp", ("role", "fsdp")),
            P("dp", None),
            P("dp", ("role", "fsdp"), None, None, None),
            P("dp", "fsdp", None, None, None),
        ),
        out_specs=(P("dp", ("role", "fsdp")), P("dp", ("role", "fsdp"), None, None, None)),
        check_vma=False,
    )
```
